256 devices in a mesh: cluster: 8 (over z), view: 32 (over y, x, core).
Axes of the slice: x: 4, y: 4, z: 8, core: 2. Of those that a mesh axis runs over, the one named last changes fastest.
Arguments:
- latents: bfloat16 [8, 32, 128, 1024], P('cluster', 'view'), may hold values from -6 to 6
- gain: float32 [1024], replicated, may hold values from 0.1 to 1.9
- w_query: bfloat16 [1024, 1024], replicated, may hold values from -2 to 2
- w_key: bfloat16 [1024, 1024], replicated, may hold values from -2 to 2
- w_value: bfloat16 [1024, 1024], replicated, may hold values from -0.1875 to 0.1875
- w_out: bfloat16 [1024, 1024], replicated, may hold values from -0.1875 to 0.1875
- pair_list: int32 [512, 3], replicated, may hold values from 0 to 255, as said below
Outputs:
- attended: bfloat16 [8, 32, 128, 1024], P('cluster', 'view')
The draws below stay inside these ranges and needn't reach their ends.
Inputs may be any that keep to these rules, and one draw needn't show every extreme that they name: `pair_list`: each row holds two different views, either in the same cluster at positions that differ by 1 to 3 (wrapping around the cluster), or at the same position in neighbouring clusters (wrapping); the third entry equals one of the two. No pair stands twice, in either order.
All inputs are finite; a program needn't handle non-finite values.
Results may differ from the reference program's by a relative error of at most 0.014.
Values may be sent and summed in bfloat16 or wider, within the bound.
A program may use at most 128 MiB of HBM per device.

```python
import math
from functools import reduce
import jax
import jax.numpy as jnp
from jax import lax

D = 1024
HEADS = 16
HEAD_DIM = 64
TOK = 128
KOFF = 3
CLUSTERS = 8
VIEWS_C = 32
VIEWS = 256
PAIRS = 512


def common_weight(key, strong, second, weak):
    key_base, key_first, key_next, key_weak = jax.random.split(key, 4)
    base = jax.random.truncated_normal(key_base, -6.0, 6.0, (D, D), jnp.float32)
    first = jax.random.randint(key_first, (), 0, HEADS)
    following = (first + 1 + jax.random.randint(key_next, (), 0, HEADS - 1)) % HEADS
    spread = jnp.exp(jax.random.uniform(key_weak, (HEADS,), jnp.float32, 0.0, math.log(weak)))
    head_ids = jnp.arange(D, dtype=jnp.int32) // HEAD_DIM
    column = jnp.where(head_ids == first, jnp.float32(strong), jnp.where(head_ids == following, jnp.float32(second), spread[head_ids]))
    return (base, column)


def draw_w_query(key, part):
    base, column = common_weight(key, 1.0, 1.0, 1.0)
    return jnp.clip(base * column[None, :] * D ** (-0.5), -2.0, 2.0).astype(jnp.bfloat16)


def draw_w_key(key, part):
    base, column = common_weight(key, 1.0, 1.0, 1.0)
    key = jax.random.fold_in(key, 23)
    other = jax.random.truncated_normal(key, -6.0, 6.0, (D, D), jnp.float32)
    return jnp.clip(other * column[None, :] * D ** (-0.5), -2.0, 2.0).astype(jnp.bfloat16)


def draw_latents(key, part):
    key = jax.random.fold_in(key, 31)
    key_base = jax.random.fold_in(key, 0)
    base = jax.random.truncated_normal(key_base, -6.0, 6.0, (CLUSTERS, VIEWS_C, TOK, D), jnp.float32)
    return base.astype(jnp.bfloat16)


def draw_pair_list(key, part):
    key = jax.random.fold_in(key, 11)
    key_order, key_side = jax.random.split(key)
    order = jax.random.permutation(key_order, (KOFF + 1) * VIEWS)[:PAIRS].astype(jnp.int32)
    view_id = order // (KOFF + 1)
    kind = order % (KOFF + 1)
    group = view_id // VIEWS_C
    place = view_id % VIEWS_C
    within = group * VIEWS_C + (place + kind + 1) % VIEWS_C
    across = (group + 1) % CLUSTERS * VIEWS_C + place
    other = jnp.where(kind < KOFF, within, across)
    side = jax.random.randint(key_side, (PAIRS,), 0, 2)
    device_id = jnp.where(side == 0, view_id, other)
    return jnp.stack([view_id, other, device_id], axis=1).astype(jnp.int32)


def noise(stream_key, shape, deviation, reach, kind=jnp.bfloat16):
    return jnp.clip(deviation * jax.random.normal(stream_key, shape, jnp.float32), -reach, reach).astype(kind)


def setup_inputs(seed: int = 0) -> dict:
    seeds = jax.random.split(jax.random.key(seed), 8)
    latents = draw_latents(jax.random.fold_in(seeds[7], 71), 0)
    gain = jnp.clip(1.0 + 0.18 * jax.random.normal(seeds[1], (D,), jnp.float32), 0.1, 1.9)
    w_query = draw_w_query(jax.random.fold_in(seeds[7], 71), 0)
    w_key = draw_w_key(jax.random.fold_in(seeds[7], 71), 0)
    w_value = noise(seeds[4], (D, D), D ** -0.5, 0.1875)
    w_out = noise(seeds[5], (D, D), D ** -0.5, 0.1875)
    pair_list = draw_pair_list(jax.random.fold_in(seeds[7], 71), 0)
    return {"latents": latents, "gain": gain, "w_query": w_query, "w_key": w_key, "w_value": w_value, "w_out": w_out, "pair_list": pair_list}


def attend_block(query, keys, values):
    tok_rows = query.shape[0]
    query_h = query.reshape(tok_rows, HEADS, HEAD_DIM).astype(jnp.float32)
    keys_h = keys.reshape(tok_rows, HEADS, HEAD_DIM).astype(jnp.float32)
    values_h = values.reshape(tok_rows, HEADS, HEAD_DIM).astype(jnp.float32)
    scores = jnp.einsum('qhe,khe->hqk', query_h, keys_h) * HEAD_DIM ** (-0.5)
    top = lax.optimization_barrier(jnp.max(scores, axis=2))
    probs = jnp.exp(scores - top[:, :, None])
    total = lax.optimization_barrier(jnp.sum(probs, axis=2))
    block = jnp.einsum('hqk,khe->qhe', probs.astype(jnp.bfloat16).astype(jnp.float32), values_h)
    return (block, top, total)

def combine_blocks(blocks):
    tops = [jnp.where(flag, part[1], jnp.float32(-1e+30)) for part, flag in blocks]
    peak = reduce(jnp.maximum, tops)
    mixed_sum = jnp.zeros_like(blocks[0][0][0])
    total_sum = jnp.zeros_like(peak)
    for (part, flag), block_top in zip(blocks, tops):
        weight = jnp.where(flag, jnp.exp(block_top - peak), jnp.float32(0.0))
        mixed_sum = mixed_sum + part[0] * weight.T[:, :, None]
        total_sum = total_sum + part[2] * weight
    merged = mixed_sum / total_sum.T[:, :, None]
    return merged.reshape(merged.shape[0], D).astype(jnp.bfloat16)

def reference(latents, gain, w_query, w_key, w_value, w_out, pair_list):
    flat = latents.reshape(VIEWS * TOK, D).astype(jnp.float32)
    mean = lax.optimization_barrier(jnp.mean(flat, axis=1, keepdims=True))
    var = lax.optimization_barrier(jnp.mean((flat - mean) ** 2, axis=1, keepdims=True))
    normed = ((flat - mean) * lax.rsqrt(var + 1e-05) * gain).astype(jnp.bfloat16)
    query_all = jnp.dot(normed, w_query, preferred_element_type=jnp.float32).astype(jnp.bfloat16).reshape(VIEWS, TOK, D)
    keys_all = jnp.dot(normed, w_key, preferred_element_type=jnp.float32).astype(jnp.bfloat16).reshape(VIEWS, TOK, D)
    values_all = jnp.dot(normed, w_value, preferred_element_type=jnp.float32).astype(jnp.bfloat16).reshape(VIEWS, TOK, D)
    first = pair_list[:, 0].astype(jnp.int32)
    second = pair_list[:, 1].astype(jnp.int32)
    adjacency = jnp.zeros((VIEWS, VIEWS), jnp.int32).at[first, second].set(1).at[second, first].set(1)

    def one_view(index):
        group = index // VIEWS_C
        place = index % VIEWS_C
        partner_ids = []
        for step in range(1, KOFF + 1):
            partner_ids.append(group * VIEWS_C + (place + step) % VIEWS_C)
        for step in range(1, KOFF + 1):
            partner_ids.append(group * VIEWS_C + (place - step) % VIEWS_C)
        partner_ids.append((group + 1) % CLUSTERS * VIEWS_C + place)
        partner_ids.append((group - 1) % CLUSTERS * VIEWS_C + place)
        query = query_all[index]
        blocks = [(attend_block(query, keys_all[index], values_all[index]), True)]
        for other in partner_ids:
            blocks.append((attend_block(query, keys_all[other], values_all[other]), adjacency[index, other] > 0))
        return combine_blocks(blocks)
    merged = lax.map(one_view, jnp.arange(VIEWS, dtype=jnp.int32))
    result = jnp.dot(merged.reshape(VIEWS * TOK, D), w_out, preferred_element_type=jnp.float32)
    return result.astype(jnp.bfloat16).reshape(CLUSTERS, VIEWS_C, TOK, D)
```

```python
import functools
import jax
import jax.numpy as jnp
from jax import lax
from jax.experimental import pallas as pl
from jax.experimental.pallas import tpu as pltpu
from jax.sharding import PartitionSpec as P

MESH = pl.DeviceIdType.MESH
BF = jnp.bfloat16
F32 = jnp.float32
TOK, D, PAIR, NP = 128, 1024, 128, 8
GA, GB, GC, GD, GE = range(5)
NONE = -1e30
COMM = True


def dot(a, b):
    return jnp.dot(a, b, preferred_element_type=F32)


def kernel(lat_hbm, gain_hbm, wq_hbm, wk_hbm, wv_hbm, wo_hbm, pl_hbm, out_hbm,
           raw, gain, wq, wkv, wo, plist, own, xb, xc, xe, kbuf, vt, qt, acc, mx, tot, bias, mg, outv,
           lsem, wsem, osem, ssem, rsem, ack):
    c = lax.axis_index("cluster")
    i = lax.axis_index("view")
    s = 1 - 2 * lax.rem(i, 2)

    def at(k):
        return lax.rem(i + k * s + 64, 32)

    sib, va, vb, vf, vg, ve = at(1), at(-1), at(3), at(2), at(-2), at(-3)
    zp, zm = lax.rem(c + 1, 8), lax.rem(c + 7, 8)

    def load(src, dst, sem):
        cp = pltpu.make_async_copy(src, dst, sem)
        cp.start()
        return cp

    l_raw = load(lat_hbm, raw, lsem.at[0])
    l_gain = load(gain_hbm, gain, lsem.at[1])
    l_kv = []
    for p in range(NP):
        cols = pl.ds(p * PAIR, PAIR)
        l_kv.append((load(wk_hbm.at[:, cols], wkv.at[p, :, pl.ds(0, PAIR)], wsem.at[2 * p]),
                     load(wv_hbm.at[:, cols], wkv.at[p, :, pl.ds(PAIR, PAIR)], wsem.at[2 * p + 1])))
    l_q = load(wq_hbm, wq, lsem.at[2])
    l_pl = load(pl_hbm, plist, lsem.at[3])
    l_o = load(wo_hbm, wo, lsem.at[4])

    if COMM:
        bar = pltpu.get_barrier_semaphore()
        count = jnp.int32(0)
        peers = [(c, sib), (c, va), (c, vb), (c, vf), (c, vg), (zp, i), (zm, i)]
        for k, (pc, pi) in enumerate(peers):
            mine = (pc > c) if k >= 5 else (pi > i)

            @pl.when(mine)
            def _():
                pl.semaphore_signal(bar, inc=1, device_id=(pc, pi), device_id_type=MESH)
            count = count + jnp.where(mine, 0, 1).astype(jnp.int32)

    vt[:, :, PAIR:PAIR + 16, :] = jnp.ones((5, NP, 16, 256), BF)
    qt[...] = jnp.zeros((NP, PAIR, 256), BF)

    l_raw.wait()
    l_gain.wait()
    flat = raw[...].astype(F32)
    mean = jnp.sum(flat, axis=1, keepdims=True) * (1.0 / D)
    cen = flat - mean
    var = jnp.sum(cen * cen, axis=1, keepdims=True) * (1.0 / D)
    own[...] = (cen * lax.rsqrt(var + 1e-05) * gain[...].reshape(1, D)).astype(BF)

    def remote(src, dst, k, dev):
        return pltpu.make_async_remote_copy(src_ref=src, dst_ref=dst, send_sem=ssem.at[k], recv_sem=rsem.at[k],
                                            device_id=dev, device_id_type=MESH)

    half = TOK // 2
    r_a = [remote(own.at[pl.ds(h * half, half)], xb.at[pl.ds(h * half, half)], h, (c, va)) for h in (0, 1)]
    r_b = remote(own, xc.at[pl.ds(0, TOK)], 2, (c, vb))
    r_zp = remote(own, xc.at[pl.ds(TOK, TOK)], 3, (zp, i))
    r_zm = remote(own, xb.at[pl.ds(TOK, TOK)], 4, (zm, i))
    r_f = [remote(xb.at[pl.ds(h * half, half)], xe.at[pl.ds(h * half, half)], 5 + h, (c, vf)) for h in (0, 1)]

    def share(k, g, row, gd, rowd):
        return (remote(kbuf.at[g, :, pl.ds(row, TOK), :], kbuf.at[gd, :, pl.ds(rowd, TOK), :], 7 + 2 * k, (c, sib)),
                remote(vt.at[g, :, pl.ds(0, PAIR), pl.ds(row, TOK)], vt.at[gd, :, pl.ds(0, PAIR), pl.ds(rowd, TOK)], 8 + 2 * k, (c, sib)))

    sh_own = share(0, GA, 0, GA, TOK)
    sh_a = share(1, GB, 0, GD, 0)
    sh_b = share(2, GC, 0, GD, TOK)

    def send(copies, slot, need):
        @pl.when(need)
        def _():
            pl.semaphore_wait(ack.at[slot], 1)
        for cp in copies:
            cp.start()

    if COMM:
        @pl.when(count > 0)
        def _():
            pl.semaphore_wait(bar, count)
        for slot, dev, cond in ((0, (c, sib), sib < i), (1, (c, va), va < i), (2, (c, vb), vb < i), (3, (c, vg), vg < i),
                                (4, (zm, i), zm < c), (5, (zp, i), zp < c)):
            @pl.when(cond)
            def _():
                pl.semaphore_signal(ack.at[slot], inc=1, device_id=dev, device_id_type=MESH)

        @pl.when(zp < c)
        def _():
            r_zp.start()
        send(r_a, 1, va > i)
        send([r_b], 2, vb > i)

    def project(g, x, rows, p):
        kv = dot(x[...], wkv[p])
        kbuf[g, p, 0:rows, :] = kv[:, :PAIR].astype(BF)
        vt[g, p, 0:PAIR, 0:rows] = kv[:, PAIR:].astype(BF).T

    def attend(g, p, b1, b2, first=False):
        n = TOK if b2 is None else 2 * TOK
        st = dot(kbuf[g, p, 0:n, :], qt[p])
        mo = None if first else mx[p]
        tops = [jnp.max(st[0:TOK], axis=0, keepdims=True) + b1]
        if b2 is not None:
            tops.append(jnp.max(st[TOK:], axis=0, keepdims=True) + b2)
        if not first:
            tops.append(mo)
        m = functools.reduce(jnp.maximum, tops)
        pr = [jnp.exp(st[0:TOK] - (m - b1)).astype(BF)]
        if b2 is not None:
            pr.append(jnp.exp(st[TOK:] - (m - b2)).astype(BF))
        pt = jnp.concatenate(pr, axis=0) if len(pr) > 1 else pr[0]
        o = dot(vt[g, p, :, 0:n], pt)
        mx[p] = m
        if first:
            tot[p] = o[PAIR:PAIR + 1]
            acc[p, 0:64, :] = o[0:64, 0:TOK]
            acc[p, 64:128, :] = o[64:128, TOK:]
        else:
            al = jnp.exp(mo - m)
            tot[p] = tot[p] * al + o[PAIR:PAIR + 1]
            acc[p, 0:64, :] = acc[p, 0:64, :] * al[:, 0:TOK] + o[0:64, 0:TOK]
            acc[p, 64:128, :] = acc[p, 64:128, :] * al[:, TOK:] + o[64:128, TOK:]

    def loop(body):
        lax.fori_loop(0, NP, lambda p, _: (body(p), 0)[1], 0)

    for p in range(NP):
        l_kv[p][0].wait()
        l_kv[p][1].wait()
    loop(lambda p: project(GA, own, TOK, p))
    if COMM:
        send(sh_own, 0, sib > i)
    l_q.wait()

    def queries(p):
        q = (dot(own[...], wq[:, pl.ds(pl.multiple_of(p * PAIR, PAIR), PAIR)]).astype(BF).astype(F32) * 0.125).T.astype(BF)
        qt[p, 0:64, 0:TOK] = q[0:64]
        qt[p, 64:128, TOK:] = q[64:128]
    loop(queries)
    if COMM:
        @pl.when(zp > c)
        def _():
            pl.semaphore_wait(ack.at[4], 1)
            r_zp.start()
        send([r_zm], 5, zm > c)

    l_pl.wait()
    me = c * 32 + i
    lane = lax.broadcasted_iota(jnp.int32, (1, 128), 1)
    ids = [c * 32 + sib, c * 32 + va, zp * 32 + i, c * 32 + vb, zm * 32 + i, c * 32 + vf, c * 32 + vg, c * 32 + ve]
    code = jnp.full((1, 128), -1, jnp.int32)
    for k, other in enumerate(ids):
        code = jnp.where(lane == 2 * k, me * 256 + other, code)
        code = jnp.where(lane == 2 * k + 1, other * 256 + me, code)
    pairs = plist[:, 0:1] * 256 + plist[:, 1:2]
    hit = jnp.max(jnp.where(pairs == code, 1.0, 0.0), axis=0, keepdims=True)
    for k in range(8):
        found = jnp.max(jnp.where(lane // 2 == k, hit, 0.0), axis=1, keepdims=True)
        bias[k] = jnp.broadcast_to(jnp.where(found > 0.5, 0.0, NONE), (1, 256))
    bz = jnp.zeros((1, 256), F32)

    def recv(copies):
        if COMM:
            for cp in copies:
                cp.wait_recv()

    recv(sh_own)
    loop(lambda p: attend(GA, p, bz, bias[0], first=True))
    recv(r_a)
    if COMM:
        send(r_f, 3, vf > i)
    recv([r_zm])
    loop(lambda p: project(GB, xb, 256, p))
    if COMM:
        for cp in sh_a:
            cp.start()
    recv([r_b, r_zp])

    def step(p):
        project(GC, xc, 256, p)
        attend(GB, p, bias[1], bias[2])
    loop(step)
    if COMM:
        for cp in sh_b:
            cp.start()
    loop(lambda p: attend(GC, p, bias[3], bias[4]))
    recv(sh_a + sh_b)
    loop(lambda p: attend(GD, p, bias[5], bias[6]))
    recv(r_f)
    loop(lambda p: project(GE, xe, TOK, p))
    loop(lambda p: attend(GE, p, bias[7], None))

    def norm(p):
        inv = 1.0 / tot[p]
        top = acc[p, 0:64, :] * inv[:, 0:TOK]
        low = acc[p, 64:128, :] * inv[:, TOK:]
        mg[:, pl.ds(pl.multiple_of(p * PAIR, PAIR), PAIR)] = jnp.concatenate([top, low], axis=0).T.astype(BF)
    loop(norm)
    l_o.wait()
    for n in range(4):
        outv[:, n * 256:(n + 1) * 256] = dot(mg[...], wo[:, n * 256:(n + 1) * 256]).astype(BF)
    cp = pltpu.make_async_copy(outv, out_hbm, osem)
    cp.start()
    if COMM:
        for r in list(r_a) + [r_b, r_zp, r_zm] + list(r_f) + list(sh_own) + list(sh_a) + list(sh_b):
            r.wait_send()
    cp.wait()


def body(latents, gain, w_query, w_key, w_value, w_out, pair_list):
    V = pltpu.VMEM
    any_ = pl.BlockSpec(memory_space=pl.ANY)
    out = pl.pallas_call(
        kernel,
        out_shape=jax.ShapeDtypeStruct((TOK, D), BF),
        in_specs=[any_] * 7,
        out_specs=any_,
        scratch_shapes=[
            V((TOK, D), BF), V((D,), F32), V((D, D), BF), V((NP, D, 256), BF), V((D, D), BF), V((512, 3), jnp.int32),
            V((TOK, D), BF), V((256, D), BF), V((256, D), BF), V((TOK, D), BF),
            V((5, NP, 256, PAIR), BF), V((5, NP, PAIR + 16, 256), BF), V((NP, PAIR, 256), BF),
            V((NP, PAIR, TOK), F32), V((NP, 1, 256), F32), V((NP, 1, 256), F32), V((8, 1, 256), F32),
            V((TOK, D), BF), V((TOK, D), BF),
            pltpu.SemaphoreType.DMA((5,)), pltpu.SemaphoreType.DMA((16,)), pltpu.SemaphoreType.DMA,
            pltpu.SemaphoreType.DMA((13,)), pltpu.SemaphoreType.DMA((13,)), pltpu.SemaphoreType.REGULAR((6,)),
        ],
        compiler_params=pltpu.CompilerParams(collective_id=0 if COMM else None, has_side_effects=True, vmem_limit_bytes=48 * 2**20),
    )(latents.reshape(TOK, D), gain, w_query, w_key, w_value, w_out, pair_list)
    return out.reshape(1, 1, TOK, D)


def solution(mesh):
    in_specs = (P("cluster", "view", None, None), P(), P(), P(), P(), P(), P())
    out_specs = P("cluster", "view", None, None)
    return jax.shard_map(body, mesh=mesh, in_specs=in_specs, out_specs=out_specs, check_vma=False)
```

```python
import functools
import jax
import jax.numpy as jnp
from jax import lax
from jax.experimental import pallas as pl
from jax.experimental.pallas import tpu as pltpu
from jax.sharding import PartitionSpec as P

MESH = pl.DeviceIdType.MESH
BF = jnp.bfloat16
F32 = jnp.float32
TOK, D, PAIR, NP = 128, 1024, 128, 8
GA, GB, GZ, GD, GE = range(5)
NONE = -1e30
COMM = True
SKIP = ""
SENDS = "abzZfs"
PIPE = True
UN = 8


def dot(a, b):
    return jnp.dot(a, b, preferred_element_type=F32)


def kernel(lat_hbm, gain_hbm, wq_hbm, wk_hbm, wv_hbm, wo_hbm, pl_hbm, out_hbm,
           raw, gain, wq, wkv, wo, plist, own, xb, xz, xe, kbuf, vt, qt, acc, mx, tot, bias, mg, outv,
           lsem, wsem, osem, ssem, rsem, ack):
    c = lax.axis_index("cluster")
    i = lax.axis_index("view")
    s = 1 - 2 * lax.rem(i, 2)

    def at(k):
        return lax.rem(i + k * s + 64, 32)

    sib, va, vb, vf, vg, ve = at(1), at(-1), at(3), at(2), at(-2), at(-3)
    zp, zm = lax.rem(c + 1, 8), lax.rem(c + 7, 8)

    if COMM:
        bar = pltpu.get_barrier_semaphore()
        count = jnp.int32(0)
        peers = [(c, sib), (c, va), (c, vb), (c, vf), (c, vg), (zp, i), (zm, i)]
        for k, (pc, pi) in enumerate(peers):
            mine = (pc > c) if k >= 5 else (pi > i)

            @pl.when(mine)
            def _():
                pl.semaphore_signal(bar, inc=1, device_id=(pc, pi), device_id_type=MESH)
            count = count + jnp.where(mine, 0, 1).astype(jnp.int32)

    def load(src, dst, sem):
        cp = pltpu.make_async_copy(src, dst, sem)
        cp.start()
        return cp

    l_raw = load(lat_hbm, raw, lsem.at[0])
    l_gain = load(gain_hbm, gain, lsem.at[1])
    l_kv = []
    for p in range(NP):
        cols = pl.ds(p * PAIR, PAIR)
        l_kv.append((load(wk_hbm.at[:, cols], wkv.at[p, :, pl.ds(0, PAIR)], wsem.at[2 * p]),
                     load(wv_hbm.at[:, cols], wkv.at[p, :, pl.ds(PAIR, PAIR)], wsem.at[2 * p + 1])))
    l_q = load(wq_hbm, wq, lsem.at[2])
    l_pl = load(pl_hbm, plist, lsem.at[3])
    l_o = load(wo_hbm, wo, lsem.at[4])

    if COMM:
        @pl.when(count > 0)
        def _():
            pl.semaphore_wait(bar, count)
        for slot, dev, cond in ((0, (c, sib), sib < i), (1, (c, va), va < i), (2, (c, vb), vb < i), (3, (c, vg), vg < i),
                                (4, (zm, i), zm < c), (5, (zp, i), zp < c)):
            @pl.when(cond)
            def _():
                pl.semaphore_signal(ack.at[slot], inc=1, device_id=dev, device_id_type=MESH)

    vt[:, :, PAIR:PAIR + 16, :] = jnp.ones((5, NP, 16, 256), BF)
    qt[...] = jnp.zeros((NP, PAIR, 256), BF)

    l_raw.wait()
    l_gain.wait()
    flat = raw[...].astype(F32)
    mean = jnp.sum(flat, axis=1, keepdims=True) * (1.0 / D)
    cen = flat - mean
    var = jnp.sum(cen * cen, axis=1, keepdims=True) * (1.0 / D)
    own[...] = (cen * lax.rsqrt(var + 1e-05) * gain[...].reshape(1, D)).astype(BF)

    class Nop:
        def start(self): pass
        def wait(self): pass
        def wait_send(self): pass
        def wait_recv(self): pass

    names = "aabzZffssssss"

    def remote(src, dst, k, dev):
        if names[k] not in SENDS:
            return Nop()
        return pltpu.make_async_remote_copy(src_ref=src, dst_ref=dst, send_sem=ssem.at[k], recv_sem=rsem.at[k],
                                            device_id=dev, device_id_type=MESH)

    half = TOK // 2
    r_a = [remote(own.at[pl.ds(h * half, half)], xb.at[pl.ds(h * half, half)], h, (c, va)) for h in (0, 1)]
    r_b = remote(own, xb.at[pl.ds(TOK, TOK)], 2, (c, vb))
    r_zp = remote(own, xz.at[pl.ds(TOK, TOK)], 3, (zp, i))
    r_zm = remote(own, xz.at[pl.ds(0, TOK)], 4, (zm, i))
    r_f = [remote(xb.at[pl.ds(h * half, half)], xe.at[pl.ds(h * half, half)], 5 + h, (c, vf)) for h in (0, 1)]

    def share(k, g, row, gd, rowd):
        return (remote(kbuf.at[g, :, pl.ds(row, TOK), :], kbuf.at[gd, :, pl.ds(rowd, TOK), :], 7 + 2 * k, (c, sib)),
                remote(vt.at[g, :, pl.ds(0, PAIR), pl.ds(row, TOK)], vt.at[gd, :, pl.ds(0, PAIR), pl.ds(rowd, TOK)], 8 + 2 * k, (c, sib)))

    sh_own = share(0, GA, 0, GA, TOK)
    sh_a = share(1, GB, 0, GD, 0)
    sh_b = share(2, GB, TOK, GD, TOK)

    def send(copies, slot, need):
        @pl.when(need)
        def _():
            pl.semaphore_wait(ack.at[slot], 1)
        for cp in copies:
            cp.start()

    def send_if(copy, need):
        @pl.when(need)
        def _():
            copy.start()

    if COMM:
        send(r_a, 1, va > i)
        send_if(r_zp, zp < c)
        send_if(r_zm, zm < c)
        send_if(r_b, vb < i)

    def project(g, x, row, rows, p):
        kv = dot(x[...], wkv[p])
        kbuf[g, p, row:row + rows, :] = kv[:, :PAIR].astype(BF)
        vt[g, p, 0:PAIR, row:row + rows] = kv[:, PAIR:].astype(BF).T

    def scores(g, p, n):
        return dot(kbuf[g, p, 0:n, :], qt[p])

    def finish(st, g, p, bs, first):
        n = st.shape[0]
        mo = None if first else mx[p]
        tops = [jnp.max(st[k * TOK:(k + 1) * TOK], axis=0, keepdims=True) + b for k, b in enumerate(bs)]
        if not first:
            tops.append(mo)
        m = functools.reduce(jnp.maximum, tops)
        pr = [jnp.exp(st[k * TOK:(k + 1) * TOK] - (m - b)).astype(BF) for k, b in enumerate(bs)]
        pt = jnp.concatenate(pr, axis=0) if len(pr) > 1 else pr[0]
        o = dot(vt[g, p, :, 0:n], pt)
        mx[p] = m
        if first:
            tot[p] = o[PAIR:PAIR + 1]
            acc[p, 0:64, :] = o[0:64, 0:TOK]
            acc[p, 64:128, :] = o[64:128, TOK:]
        else:
            al = jnp.exp(mo - m)
            tot[p] = tot[p] * al + o[PAIR:PAIR + 1]
            acc[p, 0:64, :] = acc[p, 0:64, :] * al[:, 0:TOK] + o[0:64, 0:TOK]
            acc[p, 64:128, :] = acc[p, 64:128, :] * al[:, TOK:] + o[64:128, TOK:]

    def attend(tag, g, bs, first=False, beside=None):
        if tag in SKIP:
            return
        n = TOK * len(bs)
        if PIPE:
            st = scores(g, 0, n)
            for p in range(NP):
                nxt = scores(g, p + 1, n) if p + 1 < NP else None
                if beside:
                    beside(p)
                finish(st, g, p, bs, first)
                st = nxt
        else:
            for p in range(NP):
                if beside:
                    beside(p)
                finish(scores(g, p, n), g, p, bs, first)

    def loop(body, tag=""):
        if tag and tag in SKIP:
            return
        if UN == 8:
            for p in range(NP):
                body(p)
        else:
            lax.fori_loop(0, NP, lambda p, _: (body(p), 0)[1], 0, unroll=UN)

    for p in range(NP):
        l_kv[p][0].wait()
        l_kv[p][1].wait()
    loop(lambda p: project(GA, own, 0, TOK, p), "a")
    if COMM:
        send(sh_own, 0, sib > i)

        @pl.when(vb > i)
        def _():
            pl.semaphore_wait(ack.at[2], 1)
            r_b.start()
    l_q.wait()

    def queries(p):
        q = (dot(own[...], wq[:, pl.ds(pl.multiple_of(p * PAIR, PAIR), PAIR)]).astype(BF).astype(F32) * 0.125).T.astype(BF)
        qt[p, 0:64, 0:TOK] = q[0:64]
        qt[p, 64:128, TOK:] = q[64:128]
    loop(queries, "q")
    if COMM:
        @pl.when(zp > c)
        def _():
            pl.semaphore_wait(ack.at[4], 1)
            r_zp.start()

    l_pl.wait()
    me = c * 32 + i
    first, second = plist[0:1, :], plist[1:2, :]
    ids = [c * 32 + sib, c * 32 + va, zp * 32 + i, c * 32 + vb, zm * 32 + i, c * 32 + vf, c * 32 + vg, c * 32 + ve]
    for k, other in enumerate(ids):
        match = ((first == me) & (second == other)) | ((first == other) & (second == me))
        found = jnp.max(jnp.where(match, 1.0, 0.0), axis=1, keepdims=True)
        bias[k] = jnp.broadcast_to(jnp.where(found > 0.5, 0.0, NONE), (1, 256))
    bz = jnp.zeros((1, 256), F32)

    def recv(copies):
        if COMM:
            for cp in copies:
                cp.wait_recv()

    if COMM:
        @pl.when(vf > i)
        def _():
            pl.semaphore_wait(ack.at[3], 1)
        for h in (0, 1):
            r_a[h].wait_recv()
            r_f[h].start()
    recv(sh_own)
    attend("A", GA, [bz, bias[0]], True, lambda p: project(GB, xb.at[pl.ds(0, TOK)], 0, TOK, p))
    if COMM:
        for cp in sh_a:
            cp.start()

        @pl.when(zm > c)
        def _():
            pl.semaphore_wait(ack.at[5], 1)
            r_zm.start()
    recv([r_b])
    loop(lambda p: project(GB, xb.at[pl.ds(TOK, TOK)], TOK, TOK, p), "b")
    if COMM:
        for cp in sh_b:
            cp.start()
    attend("B", GB, [bias[1], bias[3]])
    recv(sh_a + sh_b)
    recv([r_zm, r_zp])
    attend("D", GD, [bias[5], bias[6]], False, lambda p: project(GZ, xz, 0, 256, p))
    recv(r_f)
    attend("Z", GZ, [bias[2], bias[4]], False, lambda p: project(GE, xe, 0, TOK, p))
    attend("E", GE, [bias[7]])

    def norm(p):
        inv = 1.0 / tot[p]
        top = acc[p, 0:64, :] * inv[:, 0:TOK]
        low = acc[p, 64:128, :] * inv[:, TOK:]
        mg[:, pl.ds(pl.multiple_of(p * PAIR, PAIR), PAIR)] = jnp.concatenate([top, low], axis=0).T.astype(BF)
    loop(norm, "n")
    l_o.wait()
    for n in range(0 if 'o' in SKIP else 4):
        outv[:, n * 256:(n + 1) * 256] = dot(mg[...], wo[:, n * 256:(n + 1) * 256]).astype(BF)
    cp = pltpu.make_async_copy(outv, out_hbm, osem)
    cp.start()
    if COMM:
        for r in list(r_a) + [r_b, r_zp, r_zm] + list(r_f) + list(sh_own) + list(sh_a) + list(sh_b):
            r.wait_send()
    cp.wait()


def body(latents, gain, w_query, w_key, w_value, w_out, pair_list):
    V = pltpu.VMEM
    any_ = pl.BlockSpec(memory_space=pl.ANY)
    out = pl.pallas_call(
        kernel,
        out_shape=jax.ShapeDtypeStruct((TOK, D), BF),
        in_specs=[any_] * 7,
        out_specs=any_,
        scratch_shapes=[
            V((TOK, D), BF), V((D,), F32), V((D, D), BF), V((NP, D, 256), BF), V((D, D), BF), V((3, 512), jnp.int32),
            V((TOK, D), BF), V((256, D), BF), V((256, D), BF), V((TOK, D), BF),
            V((5, NP, 256, PAIR), BF), V((5, NP, PAIR + 16, 256), BF), V((NP, PAIR, 256), BF),
            V((NP, PAIR, TOK), F32), V((NP, 1, 256), F32), V((NP, 1, 256), F32), V((8, 1, 256), F32),
            V((TOK, D), BF), V((TOK, D), BF),
            pltpu.SemaphoreType.DMA((5,)), pltpu.SemaphoreType.DMA((16,)), pltpu.SemaphoreType.DMA,
            pltpu.SemaphoreType.DMA((13,)), pltpu.SemaphoreType.DMA((13,)), pltpu.SemaphoreType.REGULAR((6,)),
        ],
        compiler_params=pltpu.CompilerParams(collective_id=0 if COMM else None, has_side_effects=True, vmem_limit_bytes=62 * 2**20),
    )(latents.reshape(TOK, D), gain, w_query, w_key, w_value, w_out, pair_list.T)
    return out.reshape(1, 1, TOK, D)


def solution(mesh):
    in_specs = (P("cluster", "view", None, None), P(), P(), P(), P(), P(), P())
    out_specs = P("cluster", "view", None, None)
    return jax.shard_map(body, mesh=mesh, in_specs=in_specs, out_specs=out_specs, check_vma=False)
```

```python
import functools
import jax
import jax.numpy as jnp
from jax import lax
from jax.experimental import pallas as pl
from jax.experimental.pallas import tpu as pltpu
from jax.sharding import PartitionSpec as P

MESH = pl.DeviceIdType.MESH
BF = jnp.bfloat16
F32 = jnp.float32
TOK, D, PAIR, NP = 128, 1024, 128, 8
GA, GB, GZ, GD, GE = range(5)
NONE = -1e30
COMM = True
SKIP = ""
SENDS = "abzZfs"
DEP = 2
DEPE = 2
LATEB = True
COPYK = False
XDOT = False
VL = 62 * 2**20
UN = 8


def dot(a, b):
    return jnp.dot(a, b, preferred_element_type=F32)


def kernel(lat_hbm, gain_hbm, wq_hbm, wk_hbm, wv_hbm, wo_hbm, pl_hbm, out_hbm,
           raw, gain, wq, wkv, wo, plist, own, xb, xz, xe, kbuf, vt, qt, acc, mx, tot, bias, mg, outv,
           lsem, wsem, osem, ssem, rsem, ack):
    c = lax.axis_index("cluster")
    i = lax.axis_index("view")
    s = 1 - 2 * lax.rem(i, 2)

    def at(k):
        return lax.rem(i + k * s + 64, 32)

    sib, va, vb, vf, vg, ve = at(1), at(-1), at(3), at(2), at(-2), at(-3)
    zp, zm = lax.rem(c + 1, 8), lax.rem(c + 7, 8)

    peers = [(c, sib), (c, va), (c, vb), (c, vf), (c, vg), (zp, i), (zm, i)]
    x = lax.rem(i // 2, 4)
    roles = []
    for k, (pc, pi) in enumerate(peers):
        if k < 5:
            px = lax.rem(pi // 2, 4)
            roles.append(((x == 0) & (px == 3), (x == 3) & (px == 0)))
        else:
            roles.append((pc > c, pc < c))
    opens = [r[0] for r in roles]

    if COMM:
        bar = pltpu.get_barrier_semaphore()
        count = jnp.int32(0)
        for (pc, pi), (mine, later) in zip(peers, roles):
            @pl.when(jnp.logical_not(later))
            def _():
                pl.semaphore_signal(bar, inc=1, device_id=(pc, pi), device_id_type=MESH)
            count = count + jnp.where(mine, 0, 1).astype(jnp.int32)

    def load(src, dst, sem):
        cp = pltpu.make_async_copy(src, dst, sem)
        cp.start()
        return cp

    l_raw = load(lat_hbm, raw, lsem.at[0])
    l_gain = load(gain_hbm, gain, lsem.at[1])
    l_kv = []
    for p in range(NP):
        cols = pl.ds(p * PAIR, PAIR)
        l_kv.append((load(wk_hbm.at[:, cols], wkv.at[p, :, pl.ds(0, PAIR)], wsem.at[2 * p]),
                     load(wv_hbm.at[:, cols], wkv.at[p, :, pl.ds(PAIR, PAIR)], wsem.at[2 * p + 1])))
    l_q = load(wq_hbm, wq, lsem.at[2])
    l_pl = load(pl_hbm, plist, lsem.at[3])
    l_o = load(wo_hbm, wo, lsem.at[4])

    if COMM:
        @pl.when(count > 0)
        def _():
            pl.semaphore_wait(bar, count)
        for slot, k in ((0, 1), (1, 2), (2, 4), (3, 6), (4, 5)):
            @pl.when(roles[k][1])
            def _():
                pl.semaphore_signal(ack.at[slot], inc=1, device_id=peers[k], device_id_type=MESH)

    l_raw.wait()
    l_gain.wait()
    flat = raw[...].astype(F32)
    mean = jnp.sum(flat, axis=1, keepdims=True) * (1.0 / D)
    cen = flat - mean
    var = jnp.sum(cen * cen, axis=1, keepdims=True) * (1.0 / D)
    own[...] = (cen * lax.rsqrt(var + 1e-05) * gain[...].reshape(1, D)).astype(BF)

    class Nop:
        def start(self): pass
        def wait(self): pass
        def wait_send(self): pass
        def wait_recv(self): pass

    names = "aabzZffssssss"

    def remote(src, dst, k, dev):
        if names[k] not in SENDS:
            return Nop()
        return pltpu.make_async_remote_copy(src_ref=src, dst_ref=dst, send_sem=ssem.at[k], recv_sem=rsem.at[k],
                                            device_id=dev, device_id_type=MESH)

    half = TOK // 2
    r_a = [remote(own.at[pl.ds(h * half, half)], xb.at[pl.ds(h * half, half)], h, (c, va)) for h in (0, 1)]
    r_b = remote(own, xb.at[pl.ds(TOK, TOK)], 2, (c, vb))
    r_zp = remote(own, xz.at[pl.ds(TOK, TOK)], 3, (zp, i))
    r_zm = remote(own, xz.at[pl.ds(0, TOK)], 4, (zm, i))
    r_f = [remote(xb.at[pl.ds(h * half, half)], xe.at[pl.ds(h * half, half)], 5 + h, (c, vf)) for h in (0, 1)]

    def share(k, g, row, gd, rowd):
        return (remote(kbuf.at[g, :, pl.ds(row, TOK), :], kbuf.at[gd, :, pl.ds(rowd, TOK), :], 7 + 2 * k, (c, sib)),
                remote(vt.at[g, :, pl.ds(0, PAIR), pl.ds(row, TOK)], vt.at[gd, :, pl.ds(0, PAIR), pl.ds(rowd, TOK)], 8 + 2 * k, (c, sib)))

    sh_own = share(0, GA, 0, GA, TOK)
    sh_a = share(1, GB, 0, GD, 0)
    sh_b = share(2, GB, TOK, GD, TOK)

    def early(copies, k):
        @pl.when(jnp.logical_not(opens[k]))
        def _():
            for cp in copies:
                cp.start()

    def late(copies, k, slot):
        @pl.when(opens[k])
        def _():
            pl.semaphore_wait(ack.at[slot], 1)
            for cp in copies:
                cp.start()

    if COMM:
        early(r_a, 1)
        early([r_zp], 5)
        early([r_zm], 6)
        if not LATEB:
            early([r_b], 2)

    vt[:, :, PAIR:PAIR + 16, :] = jnp.ones((5, NP, 16, 256), BF)
    qt[...] = jnp.zeros((NP, PAIR, 256), BF)

    def project(g, x, row, rows, p):
        kv = dot(x[...], wkv[p])
        kbuf[g, p, row:row + rows, :] = kv[:, :PAIR].astype(BF)
        vt[g, p, 0:PAIR, row:row + rows] = kv[:, PAIR:].astype(BF).T

    def scores(g, p, n):
        return dot(kbuf[g, p, 0:n, :], qt[p])

    def finish(st, g, p, bs, first):
        n = st.shape[0]
        mo = None if first else mx[p]
        tops = [jnp.max(st[k * TOK:(k + 1) * TOK], axis=0, keepdims=True) + b for k, b in enumerate(bs)]
        if not first:
            tops.append(mo)
        m = functools.reduce(jnp.maximum, tops)
        pr = [jnp.exp(st[k * TOK:(k + 1) * TOK] - (m - b)).astype(BF) for k, b in enumerate(bs)]
        pt = jnp.concatenate(pr, axis=0) if len(pr) > 1 else pr[0]
        o = dot(vt[g, p, :, 0:n], pt)
        mx[p] = m
        if first:
            tot[p] = o[PAIR:PAIR + 1]
            acc[p, 0:64, :] = o[0:64, 0:TOK]
            acc[p, 64:128, :] = o[64:128, TOK:]
        else:
            al = jnp.exp(mo - m)
            tot[p] = tot[p] * al + o[PAIR:PAIR + 1]
            acc[p, 0:64, :] = acc[p, 0:64, :] * al[:, 0:TOK] + o[0:64, 0:TOK]
            acc[p, 64:128, :] = acc[p, 64:128, :] * al[:, TOK:] + o[64:128, TOK:]

    def attend(tag, g, bs, first=False, beside=None, ahead=DEP):
        if tag in SKIP:
            return
        n = TOK * len(bs)
        held = [scores(g, p, n) for p in range(ahead)]
        for p in range(NP):
            if p + ahead < NP:
                held.append(scores(g, p + ahead, n))
            if beside:
                beside(p)
            finish(held[p], g, p, bs, first)

    def loop(body, tag=""):
        if tag and tag in SKIP:
            return
        if UN == 8:
            for p in range(NP):
                body(p)
        else:
            lax.fori_loop(0, NP, lambda p, _: (body(p), 0)[1], 0, unroll=UN)

    for p in range(NP):
        l_kv[p][0].wait()
        l_kv[p][1].wait()
    loop(lambda p: project(GA, own, 0, TOK, p), "a")
    if COMM:
        late(r_a, 1, 0)
        if LATEB:
            early([r_b], 2)
        late([r_b], 2, 1)
        for cp in sh_own:
            cp.start()
    l_q.wait()

    def queries(p):
        q = (dot(own[...], wq[:, pl.ds(pl.multiple_of(p * PAIR, PAIR), PAIR)]).astype(BF).astype(F32) * 0.125).T.astype(BF)
        qt[p, 0:64, 0:TOK] = q[0:64]
        qt[p, 64:128, TOK:] = q[64:128]
    loop(queries, "q")
    if COMM:
        late([r_zp], 5, 3)

    l_pl.wait()
    me = c * 32 + i
    first, second = plist[0:1, :], plist[1:2, :]
    ids = [c * 32 + sib, c * 32 + va, zp * 32 + i, c * 32 + vb, zm * 32 + i, c * 32 + vf, c * 32 + vg, c * 32 + ve]
    for k, other in enumerate(ids):
        match = ((first == me) & (second == other)) | ((first == other) & (second == me))
        found = jnp.max(jnp.where(match, 1.0, 0.0), axis=1, keepdims=True)
        bias[k] = jnp.broadcast_to(jnp.where(found > 0.5, 0.0, NONE), (1, 256))
    bz = jnp.zeros((1, 256), F32)

    def recv(copies):
        if COMM:
            for cp in copies:
                cp.wait_recv()

    def norm(p):
        inv = 1.0 / tot[p]
        top = acc[p, 0:64, :] * inv[:, 0:TOK]
        low = acc[p, 64:128, :] * inv[:, TOK:]
        mg[:, pl.ds(pl.multiple_of(p * PAIR, PAIR), PAIR)] = jnp.concatenate([top, low], axis=0).T.astype(BF)
    recv(sh_own)
    attend("A", GA, [bz, bias[0]], True)
    if COMM:
        @pl.when(opens[3])
        def _():
            pl.semaphore_wait(ack.at[2], 1)
        for h in (0, 1):
            r_a[h].wait_recv()
            r_f[h].start()
    loop(lambda p: project(GB, xb.at[pl.ds(0, TOK)], 0, TOK, p), "a")
    if COMM:
        for cp in sh_a:
            cp.start()
        late([r_zm], 6, 4)
    recv([r_b])
    loop(lambda p: project(GB, xb.at[pl.ds(TOK, TOK)], TOK, TOK, p), "b")
    if COMM:
        for cp in sh_b:
            cp.start()
    attend("B", GB, [bias[1], bias[3]])
    recv(sh_a + sh_b)
    recv([r_zm, r_zp])
    attend("D", GD, [bias[5], bias[6]], False, lambda p: project(GZ, xz, 0, 256, p))
    attend("Z", GZ, [bias[2], bias[4]])
    recv(r_f)
    loop(lambda p: project(GE, xe, 0, TOK, p), "e")
    attend("E", GE, [bias[7]], ahead=DEPE)
    loop(norm, "n")
    if XDOT:
        outv[...] = mg[...]
        l_o.wait()
    else:
        l_o.wait()
        for n in range(0 if 'o' in SKIP else 4):
            outv[:, n * 256:(n + 1) * 256] = dot(mg[...], wo[:, n * 256:(n + 1) * 256]).astype(BF)
    cp = pltpu.make_async_copy(outv, out_hbm, osem)
    cp.start()
    if COMM:
        for r in list(r_a) + [r_b, r_zp, r_zm] + list(r_f) + list(sh_own) + list(sh_a) + list(sh_b):
            r.wait_send()
    cp.wait()


def finish_copy(src, dst, sem):
    parts = [pltpu.make_async_copy(src.at[pl.ds(k * 32, 32)], dst.at[pl.ds(k * 32, 32)], sem.at[k]) for k in range(4)]
    for part in parts:
        part.start()
    for part in parts:
        part.wait()


def body(latents, gain, w_query, w_key, w_value, w_out, pair_list):
    V = pltpu.VMEM
    any_ = pl.BlockSpec(memory_space=pl.ANY)
    out = pl.pallas_call(
        kernel,
        out_shape=jax.ShapeDtypeStruct((TOK, D), BF),
        in_specs=[any_] * 7,
        out_specs=any_,
        scratch_shapes=[
            V((TOK, D), BF), V((D,), F32), V((D, D), BF), V((NP, D, 256), BF), V((D, D), BF), V((3, 512), jnp.int32),
            V((TOK, D), BF), V((256, D), BF), V((256, D), BF), V((TOK, D), BF),
            V((5, NP, 256, PAIR), BF), V((5, NP, PAIR + 16, 256), BF), V((NP, PAIR, 256), BF),
            V((NP, PAIR, TOK), F32), V((NP, 1, 256), F32), V((NP, 1, 256), F32), V((8, 1, 256), F32),
            V((TOK, D), BF), V((TOK, D), BF),
            pltpu.SemaphoreType.DMA((5,)), pltpu.SemaphoreType.DMA((16,)), pltpu.SemaphoreType.DMA,
            pltpu.SemaphoreType.DMA((13,)), pltpu.SemaphoreType.DMA((13,)), pltpu.SemaphoreType.REGULAR((5,)),
        ],
        compiler_params=pltpu.CompilerParams(collective_id=0 if COMM else None, has_side_effects=True, vmem_limit_bytes=VL),
    )(latents.reshape(TOK, D), gain, w_query, w_key, w_value, w_out, pair_list.T)
    if COPYK:
        out = pl.pallas_call(
            finish_copy, out_shape=jax.ShapeDtypeStruct((TOK, D), BF), in_specs=[any_], out_specs=any_,
            scratch_shapes=[pltpu.SemaphoreType.DMA((4,))])(out)
    if XDOT:
        out = jnp.dot(out, w_out, preferred_element_type=F32).astype(BF)
    return out.reshape(1, 1, TOK, D)


def solution(mesh):
    in_specs = (P("cluster", "view", None, None), P(), P(), P(), P(), P(), P())
    out_specs = P("cluster", "view", None, None)
    return jax.shard_map(body, mesh=mesh, in_specs=in_specs, out_specs=out_specs, check_vma=False)
```

```python
import functools
import jax
import jax.numpy as jnp
from jax import lax
from jax.experimental import pallas as pl
from jax.experimental.pallas import tpu as pltpu
from jax.sharding import PartitionSpec as P

MESH = pl.DeviceIdType.MESH
BF = jnp.bfloat16
F32 = jnp.float32
TOK, D, PAIR, NP = 128, 1024, 128, 8
GA, GB, GZ, GD, GE = range(5)
NONE = -1e30
COMM = True
SKIP = ""
SENDS = "abzZfs"
DEP = 2
DEPE = 2
LATEB = True
LATEZ = False
ORDER = 1
CH = 2
COPYK = False
XDOT = False
VL = 62 * 2**20
UN = 8


def dot(a, b):
    return jnp.dot(a, b, preferred_element_type=F32)


def kernel(lat_hbm, gain_hbm, wq_hbm, wk_hbm, wv_hbm, wo_hbm, pl_hbm, out_hbm,
           raw, gain, wq, wkv, wo, plist, own, xb, xz, xe, kbuf, vt, qt, acc, mx, tot, bias, mg, outv,
           lsem, wsem, osem, ssem, rsem, ack):
    c = lax.axis_index("cluster")
    i = lax.axis_index("view")
    s = 1 - 2 * lax.rem(i, 2)

    def at(k):
        return lax.rem(i + k * s + 64, 32)

    sib, va, vb, vf, vg, ve = at(1), at(-1), at(3), at(2), at(-2), at(-3)
    zp, zm = lax.rem(c + 1, 8), lax.rem(c + 7, 8)

    peers = [(c, sib), (c, va), (c, vb), (c, vf), (c, vg), (zp, i), (zm, i)]
    x = lax.rem(i // 2, 4)
    roles = []
    for k, (pc, pi) in enumerate(peers):
        if k < 5:
            px = lax.rem(pi // 2, 4)
            roles.append(((x == 0) & (px == 3), (x == 3) & (px == 0)))
        else:
            roles.append((pc > c, pc < c))
    opens = [r[0] for r in roles]

    if COMM:
        bar = pltpu.get_barrier_semaphore()
        count = jnp.int32(0)
        for (pc, pi), (mine, later) in zip(peers, roles):
            @pl.when(jnp.logical_not(later))
            def _():
                pl.semaphore_signal(bar, inc=1, device_id=(pc, pi), device_id_type=MESH)
            count = count + jnp.where(mine, 0, 1).astype(jnp.int32)

    def load(src, dst, sem):
        cp = pltpu.make_async_copy(src, dst, sem)
        cp.start()
        return cp

    l_raw = load(lat_hbm, raw, lsem.at[0])
    l_gain = load(gain_hbm, gain, lsem.at[1])
    l_kv = []
    for p in range(NP):
        cols = pl.ds(p * PAIR, PAIR)
        l_kv.append((load(wk_hbm.at[:, cols], wkv.at[p, :, pl.ds(0, PAIR)], wsem.at[2 * p]),
                     load(wv_hbm.at[:, cols], wkv.at[p, :, pl.ds(PAIR, PAIR)], wsem.at[2 * p + 1])))
    l_q = load(wq_hbm, wq, lsem.at[2])
    l_pl = load(pl_hbm, plist, lsem.at[3])
    l_o = load(wo_hbm, wo, lsem.at[4])

    if COMM:
        @pl.when(count > 0)
        def _():
            pl.semaphore_wait(bar, count)
        for slot, k in ((0, 1), (1, 2), (2, 4), (3, 6), (4, 5)):
            @pl.when(roles[k][1])
            def _():
                pl.semaphore_signal(ack.at[slot], inc=1, device_id=peers[k], device_id_type=MESH)

    l_raw.wait()
    l_gain.wait()
    flat = raw[...].astype(F32)
    mean = jnp.sum(flat, axis=1, keepdims=True) * (1.0 / D)
    cen = flat - mean
    var = jnp.sum(cen * cen, axis=1, keepdims=True) * (1.0 / D)
    own[...] = (cen * lax.rsqrt(var + 1e-05) * gain[...].reshape(1, D)).astype(BF)

    class Nop:
        def start(self): pass
        def wait(self): pass
        def wait_send(self): pass
        def wait_recv(self): pass

    names = "aabzZffssssssaaaaffff"

    def remote(src, dst, k, dev):
        if names[k] not in SENDS:
            return Nop()
        return pltpu.make_async_remote_copy(src_ref=src, dst_ref=dst, send_sem=ssem.at[k], recv_sem=rsem.at[k],
                                            device_id=dev, device_id_type=MESH)

    half = TOK // CH
    r_a = [remote(own.at[pl.ds(h * half, half)], xb.at[pl.ds(h * half, half)], 13 + h, (c, va)) for h in range(CH)]
    r_b = remote(own, xb.at[pl.ds(TOK, TOK)], 2, (c, vb))
    r_zp = remote(own, xz.at[pl.ds(TOK, TOK)], 3, (zp, i))
    r_zm = remote(own, xz.at[pl.ds(0, TOK)], 4, (zm, i))
    r_f = [remote(xb.at[pl.ds(h * half, half)], xe.at[pl.ds(h * half, half)], 17 + h, (c, vf)) for h in range(CH)]

    def share(k, g, row, gd, rowd):
        return (remote(kbuf.at[g, :, pl.ds(row, TOK), :], kbuf.at[gd, :, pl.ds(rowd, TOK), :], 7 + 2 * k, (c, sib)),
                remote(vt.at[g, :, pl.ds(0, PAIR), pl.ds(row, TOK)], vt.at[gd, :, pl.ds(0, PAIR), pl.ds(rowd, TOK)], 8 + 2 * k, (c, sib)))

    sh_own = share(0, GA, 0, GA, TOK)
    sh_a = share(1, GB, 0, GD, 0)
    sh_b = share(2, GB, TOK, GD, TOK)

    def early(copies, k):
        @pl.when(jnp.logical_not(opens[k]))
        def _():
            for cp in copies:
                cp.start()

    def late(copies, k, slot):
        @pl.when(opens[k])
        def _():
            pl.semaphore_wait(ack.at[slot], 1)
            for cp in copies:
                cp.start()

    if COMM:
        early(r_a, 1)
        if not LATEZ:
            early([r_zp], 5)
            early([r_zm], 6)
        if not LATEB:
            early([r_b], 2)

    vt[:, :, PAIR:PAIR + 16, :] = jnp.ones((5, NP, 16, 256), BF)
    qt[...] = jnp.zeros((NP, PAIR, 256), BF)

    def project(g, x, row, rows, p):
        kv = dot(x[...], wkv[p])
        kbuf[g, p, row:row + rows, :] = kv[:, :PAIR].astype(BF)
        vt[g, p, 0:PAIR, row:row + rows] = kv[:, PAIR:].astype(BF).T

    def scores(g, p, n):
        return dot(kbuf[g, p, 0:n, :], qt[p])

    def finish(st, g, p, bs, first):
        n = st.shape[0]
        mo = None if first else mx[p]
        tops = [jnp.max(st[k * TOK:(k + 1) * TOK], axis=0, keepdims=True) + b for k, b in enumerate(bs)]
        if not first:
            tops.append(mo)
        m = functools.reduce(jnp.maximum, tops)
        pr = [jnp.exp(st[k * TOK:(k + 1) * TOK] - (m - b)).astype(BF) for k, b in enumerate(bs)]
        pt = jnp.concatenate(pr, axis=0) if len(pr) > 1 else pr[0]
        o = dot(vt[g, p, :, 0:n], pt)
        mx[p] = m
        if first:
            tot[p] = o[PAIR:PAIR + 1]
            acc[p, 0:64, :] = o[0:64, 0:TOK]
            acc[p, 64:128, :] = o[64:128, TOK:]
        else:
            al = jnp.exp(mo - m)
            tot[p] = tot[p] * al + o[PAIR:PAIR + 1]
            acc[p, 0:64, :] = acc[p, 0:64, :] * al[:, 0:TOK] + o[0:64, 0:TOK]
            acc[p, 64:128, :] = acc[p, 64:128, :] * al[:, TOK:] + o[64:128, TOK:]

    def attend(tag, g, bs, first=False, beside=None, ahead=DEP):
        if tag in SKIP:
            return
        n = TOK * len(bs)
        held = [scores(g, p, n) for p in range(ahead)]
        for p in range(NP):
            if p + ahead < NP:
                held.append(scores(g, p + ahead, n))
            if beside:
                beside(p)
            finish(held[p], g, p, bs, first)

    def loop(body, tag=""):
        if tag and tag in SKIP:
            return
        if UN == 8:
            for p in range(NP):
                body(p)
        else:
            lax.fori_loop(0, NP, lambda p, _: (body(p), 0)[1], 0, unroll=UN)

    for p in range(NP):
        l_kv[p][0].wait()
        l_kv[p][1].wait()
    loop(lambda p: project(GA, own, 0, TOK, p), "a")
    if COMM:
        late(r_a, 1, 0)
        if LATEB:
            early([r_b], 2)
        if LATEZ:
            early([r_zp], 5)
            early([r_zm], 6)
        late([r_b], 2, 1)
        for cp in sh_own:
            cp.start()
    l_q.wait()

    def queries(p):
        q = (dot(own[...], wq[:, pl.ds(pl.multiple_of(p * PAIR, PAIR), PAIR)]).astype(BF).astype(F32) * 0.125).T.astype(BF)
        qt[p, 0:64, 0:TOK] = q[0:64]
        qt[p, 64:128, TOK:] = q[64:128]
    loop(queries, "q")
    if COMM:
        late([r_zp], 5, 3)

    l_pl.wait()
    me = c * 32 + i
    first, second = plist[0:1, :], plist[1:2, :]
    ids = [c * 32 + sib, c * 32 + va, zp * 32 + i, c * 32 + vb, zm * 32 + i, c * 32 + vf, c * 32 + vg, c * 32 + ve]
    for k, other in enumerate(ids):
        match = ((first == me) & (second == other)) | ((first == other) & (second == me))
        found = jnp.max(jnp.where(match, 1.0, 0.0), axis=1, keepdims=True)
        bias[k] = jnp.broadcast_to(jnp.where(found > 0.5, 0.0, NONE), (1, 256))
    bz = jnp.zeros((1, 256), F32)

    def recv(copies):
        if COMM:
            for cp in copies:
                cp.wait_recv()

    def norm(p):
        inv = 1.0 / tot[p]
        top = acc[p, 0:64, :] * inv[:, 0:TOK]
        low = acc[p, 64:128, :] * inv[:, TOK:]
        mg[:, pl.ds(pl.multiple_of(p * PAIR, PAIR), PAIR)] = jnp.concatenate([top, low], axis=0).T.astype(BF)
    recv(sh_own)
    attend("A", GA, [bz, bias[0]], True)
    if COMM:
        @pl.when(opens[3])
        def _():
            pl.semaphore_wait(ack.at[2], 1)
        for h in range(CH):
            r_a[h].wait_recv()
            r_f[h].start()
        late([r_zm], 6, 4)
    loop(lambda p: project(GB, xb.at[pl.ds(0, TOK)], 0, TOK, p), "a")
    if COMM:
        for cp in sh_a:
            cp.start()
    recv([r_b])
    loop(lambda p: project(GB, xb.at[pl.ds(TOK, TOK)], TOK, TOK, p), "b")
    if COMM:
        for cp in sh_b:
            cp.start()
    def proj_z(p):
        project(GZ, xz, 0, 256, p)

    def proj_e(p):
        project(GE, xe, 0, TOK, p)

    if ORDER in (1, 2):
        recv([r_zm, r_zp])
        attend("B", GB, [bias[1], bias[3]], False, proj_z)
        attend("Z", GZ, [bias[2], bias[4]])
    if ORDER == 3:
        attend("B", GB, [bias[1], bias[3]])
        recv([r_zm, r_zp])
        loop(proj_z, "Z")
        attend("Z", GZ, [bias[2], bias[4]])
    if ORDER == 4:
        attend("B", GB, [bias[1], bias[3]])
        recv(sh_a + sh_b)
        recv([r_zm, r_zp])
        attend("D", GD, [bias[5], bias[6]], False, proj_z)
        recv(r_f)
        attend("Z", GZ, [bias[2], bias[4]], False, proj_e)
    if ORDER in (1, 3):
        recv(sh_a + sh_b)
        recv(r_f)
        attend("D", GD, [bias[5], bias[6]], False, proj_e)
    if ORDER == 2:
        recv(sh_a + sh_b)
        attend("D", GD, [bias[5], bias[6]])
        recv(r_f)
        loop(proj_e, "e")
    attend("E", GE, [bias[7]], ahead=DEPE)
    loop(norm, "n")
    if XDOT:
        outv[...] = mg[...]
        l_o.wait()
    else:
        l_o.wait()
        for n in range(0 if 'o' in SKIP else 4):
            outv[:, n * 256:(n + 1) * 256] = dot(mg[...], wo[:, n * 256:(n + 1) * 256]).astype(BF)
    cp = pltpu.make_async_copy(outv, out_hbm, osem)
    cp.start()
    if COMM:
        for r in list(r_a) + [r_b, r_zp, r_zm] + list(r_f) + list(sh_own) + list(sh_a) + list(sh_b):
            r.wait_send()
    cp.wait()


def finish_copy(src, dst, sem):
    parts = [pltpu.make_async_copy(src.at[pl.ds(k * 32, 32)], dst.at[pl.ds(k * 32, 32)], sem.at[k]) for k in range(4)]
    for part in parts:
        part.start()
    for part in parts:
        part.wait()


def body(latents, gain, w_query, w_key, w_value, w_out, pair_list):
    V = pltpu.VMEM
    any_ = pl.BlockSpec(memory_space=pl.ANY)
    out = pl.pallas_call(
        kernel,
        out_shape=jax.ShapeDtypeStruct((TOK, D), BF),
        in_specs=[any_] * 7,
        out_specs=any_,
        scratch_shapes=[
            V((TOK, D), BF), V((D,), F32), V((D, D), BF), V((NP, D, 256), BF), V((D, D), BF), V((3, 512), jnp.int32),
            V((TOK, D), BF), V((256, D), BF), V((256, D), BF), V((TOK, D), BF),
            V((5, NP, 256, PAIR), BF), V((5, NP, PAIR + 16, 256), BF), V((NP, PAIR, 256), BF),
            V((NP, PAIR, TOK), F32), V((NP, 1, 256), F32), V((NP, 1, 256), F32), V((8, 1, 256), F32),
            V((TOK, D), BF), V((TOK, D), BF),
            pltpu.SemaphoreType.DMA((5,)), pltpu.SemaphoreType.DMA((16,)), pltpu.SemaphoreType.DMA,
            pltpu.SemaphoreType.DMA((21,)), pltpu.SemaphoreType.DMA((21,)), pltpu.SemaphoreType.REGULAR((5,)),
        ],
        compiler_params=pltpu.CompilerParams(collective_id=0 if COMM else None, has_side_effects=True, vmem_limit_bytes=VL),
    )(latents.reshape(TOK, D), gain, w_query, w_key, w_value, w_out, pair_list.T)
    if COPYK:
        out = pl.pallas_call(
            finish_copy, out_shape=jax.ShapeDtypeStruct((TOK, D), BF), in_specs=[any_], out_specs=any_,
            scratch_shapes=[pltpu.SemaphoreType.DMA((4,))])(out)
    if XDOT:
        out = jnp.dot(out, w_out, preferred_element_type=F32).astype(BF)
    return out.reshape(1, 1, TOK, D)


def solution(mesh):
    in_specs = (P("cluster", "view", None, None), P(), P(), P(), P(), P(), P())
    out_specs = P("cluster", "view", None, None)
    return jax.shard_map(body, mesh=mesh, in_specs=in_specs, out_specs=out_specs, check_vma=False)
```

```python
import functools
import jax
import jax.numpy as jnp
from jax import lax
from jax.experimental import pallas as pl
from jax.experimental.pallas import tpu as pltpu
from jax.sharding import PartitionSpec as P

MESH = pl.DeviceIdType.MESH
BF = jnp.bfloat16
F32 = jnp.float32
TOK, D, PAIR, NP = 128, 1024, 128, 8
GA, GB, GZ, GD, GE = range(5)
NONE = -1e30
COMM = True
SKIP = ""
SENDS = "abzZfs"
DEP = 3
DEPE = 2
LATEB = True
LATEZ = False
ORDER = 1
CH = 2
COPYK = False
XDOT = False
VL = 62 * 2**20
UN = 8


def dot(a, b):
    return jnp.dot(a, b, preferred_element_type=F32)


def kernel(lat_hbm, gain_hbm, wq_hbm, wk_hbm, wv_hbm, wo_hbm, pl_hbm, out_hbm,
           raw, gain, wq, wkv, wo, plist, own, xb, xz, xe, kbuf, vt, qt, acc, mx, tot, bias, mg, outv,
           lsem, wsem, osem, ssem, rsem, ack):
    c = lax.axis_index("cluster")
    i = lax.axis_index("view")
    s = 1 - 2 * lax.rem(i, 2)

    def at(k):
        return lax.rem(i + k * s + 64, 32)

    sib, va, vb, vf, vg, ve = at(1), at(-1), at(3), at(2), at(-2), at(-3)
    zp, zm = lax.rem(c + 1, 8), lax.rem(c + 7, 8)

    peers = [(c, sib), (c, va), (c, vb), (c, vf), (c, vg), (zp, i), (zm, i)]
    x = lax.rem(i // 2, 4)
    roles = []
    for k, (pc, pi) in enumerate(peers):
        if k < 5:
            px = lax.rem(pi // 2, 4)
            roles.append(((x == 0) & (px == 3), (x == 3) & (px == 0)))
        else:
            roles.append((pc > c, pc < c))
    opens = [r[0] for r in roles]

    if COMM:
        bar = pltpu.get_barrier_semaphore()
        count = jnp.int32(0)
        for (pc, pi), (mine, later) in zip(peers, roles):
            @pl.when(jnp.logical_not(later))
            def _():
                pl.semaphore_signal(bar, inc=1, device_id=(pc, pi), device_id_type=MESH)
            count = count + jnp.where(mine, 0, 1).astype(jnp.int32)

    def load(src, dst, sem):
        cp = pltpu.make_async_copy(src, dst, sem)
        cp.start()
        return cp

    l_raw = load(lat_hbm, raw, lsem.at[0])
    l_gain = load(gain_hbm, gain, lsem.at[1])
    l_kv = []
    for p in range(NP):
        cols = pl.ds(p * PAIR, PAIR)
        l_kv.append((load(wk_hbm.at[:, cols], wkv.at[p, :, pl.ds(0, PAIR)], wsem.at[2 * p]),
                     load(wv_hbm.at[:, cols], wkv.at[p, :, pl.ds(PAIR, PAIR)], wsem.at[2 * p + 1])))
    l_q = load(wq_hbm, wq, lsem.at[2])
    l_pl = load(pl_hbm, plist, lsem.at[3])
    l_o = load(wo_hbm, wo, lsem.at[4])

    if COMM:
        @pl.when(count > 0)
        def _():
            pl.semaphore_wait(bar, count)
        for slot, k in ((0, 1), (1, 2), (2, 4), (3, 6), (4, 5)):
            @pl.when(roles[k][1])
            def _():
                pl.semaphore_signal(ack.at[slot], inc=1, device_id=peers[k], device_id_type=MESH)

    l_raw.wait()
    l_gain.wait()
    flat = raw[...].astype(F32)
    mean = jnp.sum(flat, axis=1, keepdims=True) * (1.0 / D)
    cen = flat - mean
    var = jnp.sum(cen * cen, axis=1, keepdims=True) * (1.0 / D)
    own[...] = (cen * lax.rsqrt(var + 1e-05) * gain[...].reshape(1, D)).astype(BF)

    class Nop:
        def start(self): pass
        def wait(self): pass
        def wait_send(self): pass
        def wait_recv(self): pass

    names = "aabzZffssssssaaaaffff"

    def remote(src, dst, k, dev):
        if names[k] not in SENDS:
            return Nop()
        return pltpu.make_async_remote_copy(src_ref=src, dst_ref=dst, send_sem=ssem.at[k], recv_sem=rsem.at[k],
                                            device_id=dev, device_id_type=MESH)

    half = TOK // CH
    r_a = [remote(own.at[pl.ds(h * half, half)], xb.at[pl.ds(h * half, half)], 13 + h, (c, va)) for h in range(CH)]
    r_b = remote(own, xb.at[pl.ds(TOK, TOK)], 2, (c, vb))
    r_zp = remote(own, xz.at[pl.ds(TOK, TOK)], 3, (zp, i))
    r_zm = remote(own, xz.at[pl.ds(0, TOK)], 4, (zm, i))
    r_f = [remote(xb.at[pl.ds(h * half, half)], xe.at[pl.ds(h * half, half)], 17 + h, (c, vf)) for h in range(CH)]

    def share(k, g, row, gd, rowd):
        return (remote(kbuf.at[g, :, pl.ds(row, TOK), :], kbuf.at[gd, :, pl.ds(rowd, TOK), :], 7 + 2 * k, (c, sib)),
                remote(vt.at[g, :, pl.ds(0, PAIR), pl.ds(row, TOK)], vt.at[gd, :, pl.ds(0, PAIR), pl.ds(rowd, TOK)], 8 + 2 * k, (c, sib)))

    sh_own = share(0, GA, 0, GA, TOK)
    sh_a = share(1, GB, 0, GD, 0)
    sh_b = share(2, GB, TOK, GD, TOK)

    def early(copies, k):
        @pl.when(jnp.logical_not(opens[k]))
        def _():
            for cp in copies:
                cp.start()

    def late(copies, k, slot):
        @pl.when(opens[k])
        def _():
            pl.semaphore_wait(ack.at[slot], 1)
            for cp in copies:
                cp.start()

    if COMM:
        early(r_a, 1)
        if not LATEZ:
            early([r_zp], 5)
            early([r_zm], 6)
        if not LATEB:
            early([r_b], 2)

    vt[:, :, PAIR:PAIR + 16, :] = jnp.ones((5, NP, 16, 256), BF)
    qt[...] = jnp.zeros((NP, PAIR, 256), BF)

    def project(g, x, row, rows, p):
        kv = dot(x[...], wkv[p])
        kbuf[g, p, row:row + rows, :] = kv[:, :PAIR].astype(BF)
        vt[g, p, 0:PAIR, row:row + rows] = kv[:, PAIR:].astype(BF).T

    def scores(g, p, n):
        return dot(kbuf[g, p, 0:n, :], qt[p])

    def finish(st, g, p, bs, first):
        n = st.shape[0]
        mo = None if first else mx[p]
        tops = [jnp.max(st[k * TOK:(k + 1) * TOK], axis=0, keepdims=True) + b for k, b in enumerate(bs)]
        if not first:
            tops.append(mo)
        m = functools.reduce(jnp.maximum, tops)
        pr = [jnp.exp(st[k * TOK:(k + 1) * TOK] - (m - b)).astype(BF) for k, b in enumerate(bs)]
        pt = jnp.concatenate(pr, axis=0) if len(pr) > 1 else pr[0]
        o = dot(vt[g, p, :, 0:n], pt)
        mx[p] = m
        if first:
            tot[p] = o[PAIR:PAIR + 1]
            acc[p, 0:64, :] = o[0:64, 0:TOK]
            acc[p, 64:128, :] = o[64:128, TOK:]
        else:
            al = jnp.exp(mo - m)
            tot[p] = tot[p] * al + o[PAIR:PAIR + 1]
            acc[p, 0:64, :] = acc[p, 0:64, :] * al[:, 0:TOK] + o[0:64, 0:TOK]
            acc[p, 64:128, :] = acc[p, 64:128, :] * al[:, TOK:] + o[64:128, TOK:]

    def attend(tag, g, bs, first=False, beside=None, ahead=DEP):
        if tag in SKIP:
            return
        n = TOK * len(bs)
        held = [scores(g, p, n) for p in range(ahead)]
        for p in range(NP):
            if p + ahead < NP:
                held.append(scores(g, p + ahead, n))
            if beside:
                beside(p)
            finish(held[p], g, p, bs, first)

    def loop(body, tag=""):
        if tag and tag in SKIP:
            return
        if UN == 8:
            for p in range(NP):
                body(p)
        else:
            lax.fori_loop(0, NP, lambda p, _: (body(p), 0)[1], 0, unroll=UN)

    for p in range(NP):
        l_kv[p][0].wait()
        l_kv[p][1].wait()
    loop(lambda p: project(GA, own, 0, TOK, p), "a")
    if COMM:
        for cp in sh_own:
            cp.start()
        late(r_a, 1, 0)
        if LATEB:
            early([r_b], 2)
        if LATEZ:
            early([r_zp], 5)
            early([r_zm], 6)
        late([r_b], 2, 1)
    l_q.wait()

    def queries(p):
        q = (dot(own[...], wq[:, pl.ds(pl.multiple_of(p * PAIR, PAIR), PAIR)]).astype(BF).astype(F32) * 0.125).T.astype(BF)
        qt[p, 0:64, 0:TOK] = q[0:64]
        qt[p, 64:128, TOK:] = q[64:128]
    loop(queries, "q")
    if COMM:
        late([r_zp], 5, 3)

    l_pl.wait()
    me = c * 32 + i
    first, second = plist[0:1, :], plist[1:2, :]
    ids = [c * 32 + sib, c * 32 + va, zp * 32 + i, c * 32 + vb, zm * 32 + i, c * 32 + vf, c * 32 + vg, c * 32 + ve]
    for k, other in enumerate(ids):
        match = ((first == me) & (second == other)) | ((first == other) & (second == me))
        found = jnp.max(jnp.where(match, 1.0, 0.0), axis=1, keepdims=True)
        bias[k] = jnp.broadcast_to(jnp.where(found > 0.5, 0.0, NONE), (1, 256))
    bz = jnp.zeros((1, 256), F32)

    def recv(copies):
        if COMM:
            for cp in copies:
                cp.wait_recv()

    def norm(p):
        inv = 1.0 / tot[p]
        top = acc[p, 0:64, :] * inv[:, 0:TOK]
        low = acc[p, 64:128, :] * inv[:, TOK:]
        mg[:, pl.ds(pl.multiple_of(p * PAIR, PAIR), PAIR)] = jnp.concatenate([top, low], axis=0).T.astype(BF)
    recv(sh_own)
    attend("A", GA, [bz, bias[0]], True)
    if COMM:
        @pl.when(opens[3])
        def _():
            pl.semaphore_wait(ack.at[2], 1)
        for h in range(CH):
            r_a[h].wait_recv()
            r_f[h].start()
        late([r_zm], 6, 4)
    loop(lambda p: project(GB, xb.at[pl.ds(0, TOK)], 0, TOK, p), "a")
    if COMM:
        for cp in sh_a:
            cp.start()
    recv([r_b])
    loop(lambda p: project(GB, xb.at[pl.ds(TOK, TOK)], TOK, TOK, p), "b")
    if COMM:
        for cp in sh_b:
            cp.start()
    def proj_z(p):
        project(GZ, xz, 0, 256, p)

    def proj_e(p):
        project(GE, xe, 0, TOK, p)

    if ORDER in (1, 2):
        recv([r_zm, r_zp])
        attend("B", GB, [bias[1], bias[3]], False, proj_z)
        attend("Z", GZ, [bias[2], bias[4]])
    if ORDER == 3:
        attend("B", GB, [bias[1], bias[3]])
        recv([r_zm, r_zp])
        loop(proj_z, "Z")
        attend("Z", GZ, [bias[2], bias[4]])
    if ORDER == 4:
        attend("B", GB, [bias[1], bias[3]])
        recv(sh_a + sh_b)
        recv([r_zm, r_zp])
        attend("D", GD, [bias[5], bias[6]], False, proj_z)
        recv(r_f)
        attend("Z", GZ, [bias[2], bias[4]], False, proj_e)
    if ORDER in (1, 3):
        recv(sh_a + sh_b)
        recv(r_f)
        attend("D", GD, [bias[5], bias[6]], False, proj_e)
    if ORDER == 2:
        recv(sh_a + sh_b)
        attend("D", GD, [bias[5], bias[6]])
        recv(r_f)
        loop(proj_e, "e")
    attend("E", GE, [bias[7]], ahead=DEPE)
    loop(norm, "n")
    l_o.wait()
    stores = []
    for n in range(4):
        cols = pl.ds(n * 256, 256)
        outv[:, cols] = dot(mg[...], wo[:, cols]).astype(BF)
        stores.append(pltpu.make_async_copy(outv.at[:, cols], out_hbm.at[:, cols], osem.at[n]))
        stores[-1].start()
    if COMM:
        for r in list(r_a) + [r_b, r_zp, r_zm] + list(r_f) + list(sh_own) + list(sh_a) + list(sh_b):
            r.wait_send()
    for cp in stores:
        cp.wait()


def finish_copy(src, dst, sem):
    parts = [pltpu.make_async_copy(src.at[pl.ds(k * 32, 32)], dst.at[pl.ds(k * 32, 32)], sem.at[k]) for k in range(4)]
    for part in parts:
        part.start()
    for part in parts:
        part.wait()


def body(latents, gain, w_query, w_key, w_value, w_out, pair_list):
    V = pltpu.VMEM
    any_ = pl.BlockSpec(memory_space=pl.ANY)
    out = pl.pallas_call(
        kernel,
        out_shape=jax.ShapeDtypeStruct((TOK, D), BF),
        in_specs=[any_] * 7,
        out_specs=any_,
        scratch_shapes=[
            V((TOK, D), BF), V((D,), F32), V((D, D), BF), V((NP, D, 256), BF), V((D, D), BF), V((3, 512), jnp.int32),
            V((TOK, D), BF), V((256, D), BF), V((256, D), BF), V((TOK, D), BF),
            V((5, NP, 256, PAIR), BF), V((5, NP, PAIR + 16, 256), BF), V((NP, PAIR, 256), BF),
            V((NP, PAIR, TOK), F32), V((NP, 1, 256), F32), V((NP, 1, 256), F32), V((8, 1, 256), F32),
            V((TOK, D), BF), V((TOK, D), BF),
            pltpu.SemaphoreType.DMA((5,)), pltpu.SemaphoreType.DMA((16,)), pltpu.SemaphoreType.DMA((4,)),
            pltpu.SemaphoreType.DMA((21,)), pltpu.SemaphoreType.DMA((21,)), pltpu.SemaphoreType.REGULAR((5,)),
        ],
        compiler_params=pltpu.CompilerParams(collective_id=0 if COMM else None, has_side_effects=True, vmem_limit_bytes=VL),
    )(latents.reshape(TOK, D), gain, w_query, w_key, w_value, w_out, pair_list.T)
    if COPYK:
        out = pl.pallas_call(
            finish_copy, out_shape=jax.ShapeDtypeStruct((TOK, D), BF), in_specs=[any_], out_specs=any_,
            scratch_shapes=[pltpu.SemaphoreType.DMA((4,))])(out)
    if XDOT:
        out = jnp.dot(out, w_out, preferred_element_type=F32).astype(BF)
    return out.reshape(1, 1, TOK, D)


def solution(mesh):
    in_specs = (P("cluster", "view", None, None), P(), P(), P(), P(), P(), P())
    out_specs = P("cluster", "view", None, None)
    return jax.shard_map(body, mesh=mesh, in_specs=in_specs, out_specs=out_specs, check_vma=False)
```
